512 devices in a mesh: energy: 32 (over z, core), transpor: 16 (over x, y).
Axes of the slice: x: 4, y: 4, z: 16, core: 2. Of those that a mesh axis runs over, the one named last changes fastest.
Arguments:
- energy_level: float32 [32], P('energy'), may hold values from -3 to 3
- sigma_real: float32 [32, 2048], P('energy', 'transpor'), may hold values from -1.5 to 1.5
- sigma_width: float32 [32, 2048], P('energy', 'transpor'), may hold values from 0.02 to 0.2
- onsite: float32 [16, 128, 128], P('transpor'), may hold values from -2 to 2, as said below
- coupling: float32 [16, 128, 128], P('transpor'), may hold values from -0.5 to 0.5
- source: float32 [2, 32, 16, 128, 128], P(None, 'energy', 'transpor'), may hold values from -6 to 6
- mode_strength: float32 [6], replicated, may hold values from 0.3 to 1.5
- mode_shift: int32 [6], replicated, may hold values from 1 to 10, as said below
Outputs:
- density: float32 [32, 2048], P('energy', 'transpor')
- sigma_phonon: float32 [32, 2048], P('energy', 'transpor')
The draws below stay inside these ranges and needn't reach their ends.
Inputs may be any that keep to these rules, and one draw needn't show every extreme that they name: `mode_shift`: every value lies in 1 to 10, and at least one mode has exactly 10. `onsite`: each block is a symmetric matrix.
All inputs are finite; a program needn't handle non-finite values.
Results may differ from the reference program's by a relative error of at most 0.0003.
Values sent between devices are 32-bit elements; how exact they have to be, the bound alone decides.
No kernel may reach another device: no remote copies, remote signals or barrier semaphores. Data moves between devices by JAX's collectives and lax.ppermute only.
A program may use at most 64 MiB of HBM per device.

```python
import math
import jax
import jax.numpy as jnp
from jax import lax

ORB = 128
SRC = 128
MODES = 6
ENERGIES = 32
BLOCKS = 16
SHIFT_MAX = 10


def draw_onsite(key, part):
    noise_key = jax.random.fold_in(key, 11)
    level_key = jax.random.fold_in(key, 12)
    noise = jax.random.truncated_normal(noise_key, -3.0, 3.0, (BLOCKS, ORB, ORB), jnp.float32)
    noise = noise * (0.5 / math.sqrt(ORB))
    levels = jax.random.uniform(level_key, (BLOCKS, ORB), jnp.float32, -1.0, 1.0)
    symmetric = noise + jnp.swapaxes(noise, 1, 2)
    return symmetric + levels[:, :, None] * jnp.eye(ORB, dtype=jnp.float32)


def draw_mode_shift(key, part):
    value_key = jax.random.fold_in(key, 21)
    place_key = jax.random.fold_in(key, 22)
    values = jax.random.randint(value_key, (MODES,), 1, SHIFT_MAX + 1)
    chosen = jax.random.randint(place_key, (), 0, MODES)
    return jnp.where(jnp.arange(MODES) == chosen, SHIFT_MAX, values).astype(jnp.int32)


def block_scale(stream_key, shape, shards, least, high):
    factor_of = 1.0
    for position, shards_of in shards:
        draws = jax.random.uniform(jax.random.fold_in(jax.random.fold_in(stream_key, 6), position), (shards_of,), jnp.float32, least / len(shards), high / len(shards))
        factor_of = factor_of * jnp.repeat(jnp.exp(draws), shape[position] // shards_of).reshape((-1,) + (1,) * (len(shape) - 1 - position))
    return factor_of


def bell_draw(key, dims, deviation, bound, split=(), held_as=jnp.bfloat16):
    drawn = deviation * jax.random.normal(key, dims, jnp.float32)
    if split:
        drawn = drawn * block_scale(key, dims, split, -0.22, 0.18)
    return jnp.clip(drawn, -bound, bound).astype(held_as)


def setup_inputs(seed: int = 0) -> dict:
    key_list = jax.random.split(jax.random.key(seed), 9)
    energy_level = jnp.clip(jax.random.uniform(key_list[0], (ENERGIES,), jnp.float32, -3.0, 3.0) * block_scale(key_list[0], (ENERGIES,), ((0, 32),), -0.4, 0.0), -3.0, 3.0)
    sigma_real = bell_draw(key_list[1], (ENERGIES, BLOCKS * ORB), 0.3, 1.5, ((0, 32), (1, 16)), jnp.float32)
    sigma_width = jnp.clip(jnp.exp(math.log(0.2) - 2.3025851 * jax.random.uniform(key_list[2], (ENERGIES, BLOCKS * ORB), jnp.float32) ** block_scale(key_list[2], (ENERGIES, BLOCKS * ORB), ((0, 32), (1, 16)), -0.2, 0.2)), 0.02, 0.2)
    onsite = draw_onsite(jax.random.fold_in(key_list[8], 71), 0)
    coupling = bell_draw(key_list[4], (BLOCKS, ORB, ORB), ORB ** -0.5, 0.5, ((0, 16),), jnp.float32)
    source = bell_draw(key_list[5], (2, ENERGIES, BLOCKS, ORB, SRC), 1.0, 6.0, ((1, 32), (2, 16)), jnp.float32)
    mode_strength = jnp.clip(jnp.exp(jax.random.uniform(key_list[6], (MODES,), jnp.float32, math.log(0.3), math.log(1.5))), 0.3, 1.5)
    mode_shift = draw_mode_shift(jax.random.fold_in(key_list[8], 71), 0)
    return dict(energy_level=energy_level, sigma_real=sigma_real, sigma_width=sigma_width, onsite=onsite, coupling=coupling, source=source, mode_strength=mode_strength, mode_shift=mode_shift)


broadening = 0.2
highest = lax.Precision.HIGHEST

def embed(real_part, imag_part):
    upper_half = jnp.concatenate([real_part, -imag_part], axis=-1)
    bottom = jnp.concatenate([imag_part, real_part], axis=-1)
    return jnp.concatenate([upper_half, bottom], axis=-2)

def reference(energy_level, sigma_real, sigma_width, onsite, coupling, source, mode_strength, mode_shift):
    identity = jnp.eye(ORB, dtype=jnp.float32)
    zero_block = jnp.zeros((BLOCKS, ORB, ORB), jnp.float32)
    couplings = embed(coupling, zero_block)

    def solve_energy(energy_index):
        energy_value = energy_level[energy_index]
        shifts = sigma_real[energy_index].reshape(BLOCKS, ORB)
        widths = sigma_width[energy_index].reshape(BLOCKS, ORB)
        real_part = (energy_value - shifts)[:, :, None] * identity - onsite
        imag_part = (broadening + widths)[:, :, None] * identity
        diagonal = embed(real_part, imag_part)
        sources = jnp.concatenate([source[0, energy_index], source[1, energy_index]], axis=-2)

        def forward(state_pair, inputs):
            prev_diag, prev_rhs = state_pair
            block_diag, link_block, block_rhs = inputs
            solved = jnp.linalg.solve(prev_diag, jnp.concatenate([link_block, prev_rhs], axis=-1))
            new_diag = block_diag - jnp.dot(link_block.T, solved[:, :2 * ORB], precision=highest)
            new_rhs = block_rhs + jnp.dot(link_block.T, solved[:, 2 * ORB:], precision=highest)
            return ((new_diag, new_rhs), (new_diag, new_rhs))
        start_state = (diagonal[0], sources[0])
        _, (diags, rhs_rest) = lax.scan(forward, start_state, (diagonal[1:], couplings[1:], sources[1:]))
        all_diag = jnp.concatenate([diagonal[:1], diags], axis=0)
        all_rhs = jnp.concatenate([sources[:1], rhs_rest], axis=0)
        final_block = jnp.linalg.solve(all_diag[-1], all_rhs[-1])

        def backward(following, inputs):
            block_diag, block_rhs, link_next = inputs
            result = jnp.linalg.solve(block_diag, block_rhs + jnp.dot(link_next, following, precision=highest))
            return (result, result)
        _, earlier = lax.scan(backward, final_block, (all_diag[:-1], all_rhs[:-1], couplings[1:]), reverse=True)
        solution = jnp.concatenate([earlier, final_block[None]], axis=0)
        squares = solution[:, :ORB] ** 2 + solution[:, ORB:] ** 2
        return jnp.mean(squares, axis=-1).reshape(BLOCKS * ORB)
    density = lax.map(solve_energy, jnp.arange(ENERGIES))
    row_index = jnp.arange(ENERGIES)[:, None]
    col_index = jnp.arange(ENERGIES)[None, :]
    distance = col_index - row_index
    matrix = jnp.zeros((ENERGIES, ENERGIES), jnp.float32)
    for phonon_mode in range(MODES):
        hits = (distance == mode_shift[phonon_mode]).astype(jnp.float32) + (distance == -mode_shift[phonon_mode]).astype(jnp.float32)
        matrix = matrix + mode_strength[phonon_mode] * hits
    sigma_phonon = jnp.dot(matrix, density, precision=highest)
    return (density, sigma_phonon)
```

```python
import functools

import jax
import jax.numpy as jnp
from jax import lax
from jax.experimental import pallas as pl
from jax.experimental.pallas import tpu as pltpu
from jax.sharding import PartitionSpec as P

N = 128
TILES = N // 8
HALF = 8
COLS = 16
PACK = N + 8
broadening = 0.2
prec = lax.Precision.HIGHEST
f32 = jnp.float32

GROUPS = [list(range(8)), [12, 13, 14, 15, 8, 9, 10, 11]]
MIRROR = [(x * 4 + y, (3 - x) * 4 + y) for x in range(4) for y in range(4)]


def dot(a, b, dims=((1,), (0,))):
    return lax.dot_general(a, b, (dims, ((), ())), precision=prec, preferred_element_type=f32)


def lanes_of(v, k):
    return jnp.broadcast_to(v[:, k : k + 1], (8, N))


def row_of(v, k):
    return jnp.broadcast_to(v[k : k + 1, :], (8, N))


def pack(re, im):
    return jnp.concatenate([re, im], axis=1)


def turned(v):
    return pack(-v[:, N:], v[:, :N])


def rows_for(v):
    return jnp.concatenate([v, turned(v)], axis=0)


def flip(v):
    return pack(v[:, :N].T, v[:, N:].T)


def times(a, b):
    return dot(a, rows_for(b))


def times_t(a, b):
    f = jnp.concatenate([pack(b[:, :N], -b[:, N:]), pack(b[:, N:], b[:, :N])], axis=0)
    return dot(a, f, ((1,), (1,)))


def iota(shape, d):
    return lax.broadcasted_iota(jnp.int32, shape, d)


def invert(ms, ahead=2):
    R = [[m[8 * u : 8 * u + 8, :N] for u in range(TILES)] for m in ms]
    I = [[m[8 * u : 8 * u + 8, N:] for u in range(TILES)] for m in ms]
    sub, lane = iota((8, N), 0), iota((8, N), 1)
    zero = jnp.zeros((8, 2 * N), f32)
    for t in range(TILES):
        here = (lane >= 8 * t) & (lane < 8 * t + 8)
        unit = jnp.where(lane == sub + 8 * t, 1.0, 0.0)
        for b in range(len(ms)):
            xr, xi = R[b], I[b]
            dr = [lanes_of(xr[t], 8 * t + j) for j in range(8)]
            di = [lanes_of(xi[t], 8 * t + j) for j in range(8)]
            soon = range(t + 1, min(t + 1 + ahead, TILES))
            lr = {u: [lanes_of(xr[u], 8 * t + j) for j in range(8)] for u in soon}
            li = {u: [lanes_of(xi[u], 8 * t + j) for j in range(8)] for u in soon}
            pr = jnp.where(here, unit, xr[t])
            pi = jnp.where(here, 0.0, xi[t])
            for k in range(8):
                p_r, p_i = row_of(dr[k], k), row_of(di[k], k)
                scale = 1.0 / (p_r * p_r + p_i * p_i)
                ir, ii = p_r * scale, p_i * scale
                cr = dr[k] - jnp.where(sub == k, 1.0, 0.0)
                ci = di[k]
                fr = cr * ir + ci * ii
                fi = ci * ir - cr * ii
                for j in range(k + 1, 8):
                    br, bi = row_of(dr[j], k), row_of(di[j], k)
                    dr[j] = dr[j] - fr * br + fi * bi
                    di[j] = di[j] - fr * bi - fi * br
                br, bi = row_of(pr, k), row_of(pi, k)
                pr = pr - fr * br + fi * bi
                pi = pi - fr * bi - fi * br
            new = {t: (pr, pi)}
            for u in soon:
                yr = jnp.where(here, 0.0, xr[u])
                yi = jnp.where(here, 0.0, xi[u])
                for j in range(8):
                    br, bi = row_of(pr, j), row_of(pi, j)
                    yr = yr - lr[u][j] * br + li[u][j] * bi
                    yi = yi - lr[u][j] * bi - li[u][j] * br
                new[u] = (yr, yi)
            rest = [u for u in range(TILES) if u not in new]
            left = jnp.concatenate([pack(xr[u], xi[u]) for u in rest], 0)
            top = [pack(pr, pi) if u == t else zero for u in range(TILES)]
            low = [pack(-pi, pr) if u == t else zero for u in range(TILES)]
            delta = dot(left, jnp.concatenate(top + low, 0))
            for q, u in enumerate(rest):
                new[u] = (
                    jnp.where(here, 0.0, xr[u]) - delta[8 * q : 8 * q + 8, :N],
                    jnp.where(here, 0.0, xi[u]) - delta[8 * q : 8 * q + 8, N:],
                )
            R[b] = [new[u][0] for u in range(TILES)]
            I[b] = [new[u][1] for u in range(TILES)]
    return [jnp.concatenate([pack(r, i) for r, i in zip(R[b], I[b])], 0) for b in range(len(ms))]


def fold(m):
    re, im = m[:, :N], m[:, N:]
    i, j = iota((N, N), 0), iota((N, N), 1)
    diagonal = jnp.sum(jnp.where(i == j, im, 0.0), axis=0, keepdims=True)
    return jnp.concatenate([jnp.where(i >= j, re, im), jnp.broadcast_to(diagonal, (8, N))], axis=0)


def unfold(v):
    a, diagonal = v[:N], v[N : N + 1]
    i, j = iota((N, N), 0), iota((N, N), 1)
    at = a.T
    re = jnp.where(i >= j, a, at)
    im = jnp.where(i == j, diagonal, jnp.where(i < j, a, at))
    return pack(re, im)


def prepare_kernel(side_ref, coupling_ref, source_ref, coupling_out, source_out):
    link = coupling_ref[0]
    coupling_out[...] = jnp.where(side_ref[0] == 1, link.T, link)
    for part in range(2):
        flipped = source_ref[part, 0, 0].T
        for q in range(HALF):
            source_out[q, COLS * part : COLS * (part + 1)] = flipped[COLS * q : COLS * (q + 1)]


def own_kernel(side_ref, energy_ref, shift_ref, width_ref, onsite_ref, out_ref):
    i, j = iota((N, N), 0), iota((N, N), 1)
    re = jnp.where(i == j, energy_ref[0] - shift_ref[...], 0.0) - onsite_ref[0]
    im = jnp.where(i == j, broadening + width_ref[...], 0.0)
    block = pack(re, im)

    @pl.when(side_ref[1] == 0)
    def _():
        out_ref[...] = fold(invert([block])[0])

    @pl.when(side_ref[1] == 1)
    def _():
        out_ref[...] = fold(block)


def half_kernel(side_ref, blocks_ref, first_ref, mid_ref, w_ref, y_ref):
    right = side_ref[0]
    place = [jnp.bitwise_xor(m, 3 * right) for m in range(HALF)]
    link_place = [jnp.where(right == 1, place[m], m + 1) for m in range(HALF - 1)]
    U = [first_ref[link_place[m], :N] for m in range(HALF - 1)]
    blocks = [unfold(blocks_ref[place[m]]) for m in range(HALF)]
    z = [pack(first_ref[place[m], N : N + COLS], first_ref[place[m], N + COLS :]) for m in range(HALF)]
    D = {m: blocks[m] for m in range(1, HALF, 2)}
    UT = [u.T for u in U]
    V = {}
    slot = iter(range(11))

    def keep(w):
        w_ref[next(slot)] = w

    for m in range(0, HALF, 2):
        p = blocks[m]
        stacked = jnp.concatenate([p[:, :N], p[:, N:]], axis=0)
        y_ref[m] = times(z[m], p)
        if m == 0:
            w = dot(stacked, U[0])
            wr = pack(w[:N], w[N:])
        else:
            w = dot(stacked, pack(UT[m - 1], U[m]))
            wl = pack(w[:N, :N], w[N:, :N])
            wr = pack(w[:N, N:], w[N:, N:])
            up = dot(U[m - 1], jnp.concatenate([wl, wr], axis=1))
            D[m - 1] = D[m - 1] - up[:, : 2 * N]
            V[m - 1] = up[:, 2 * N :]
            z[m - 1] = z[m - 1] + times(z[m], wl)
            keep(wl)
        D[m + 1] = D[m + 1] - dot(UT[m], wr)
        z[m + 1] = z[m + 1] + times(z[m], wr)
        keep(wr)

    p1, p5 = invert([D[1], D[5]])
    y_ref[1] = times(z[1], p1)
    y_ref[5] = times(z[5], p5)
    w1r = times(p1, V[1])
    w5l = times(p5, flip(V[3]))
    w5r = times(p5, V[5])
    D[3] = D[3] - times(flip(V[1]), w1r) - times(V[3], w5l)
    V3 = times(V[3], w5r)
    D[7] = D[7] - times(flip(V[5]), w5r)
    z[3] = z[3] + times(z[1], w1r) + times(z[5], w5l)
    z[7] = z[7] + times(z[5], w5r)
    keep(w1r)
    keep(w5l)
    keep(w5r)

    (p3,) = invert([D[3]])
    y_ref[3] = times(z[3], p3)
    w3r = times(p3, V3)
    keep(w3r)
    D[7] = D[7] - times(flip(V3), w3r)
    z[7] = z[7] + times(z[3], w3r)
    mid_ref[:PACK] = fold(D[7])
    mid_ref[PACK : PACK + COLS] = z[7][:, :N]
    mid_ref[PACK + COLS :] = z[7][:, N:]


def middle_kernel(side_ref, mine_ref, other_ref, own_link_ref, sent_link_ref, w_ref, y_ref, out_ref):
    right = side_ref[0]
    sent = sent_link_ref[...]
    U = jnp.where(right == 1, own_link_ref[...], sent.T)
    UT = jnp.where(right == 1, own_link_ref[...].T, sent)
    mine = unfold(mine_ref[:PACK])
    z = pack(mine_ref[PACK : PACK + COLS], mine_ref[PACK + COLS :])
    z_other = pack(other_ref[PACK : PACK + COLS], other_ref[PACK + COLS :])
    (q,) = invert([unfold(other_ref[:PACK])])
    w = dot(jnp.concatenate([q[:, :N], q[:, N:]], axis=0), UT)
    w = pack(w[:N], w[N:])
    z = z + times(z_other, w)
    (s,) = invert([mine - dot(U, w)])
    x = {7: times(z, s)}
    x[3] = y_ref[3] + times_t(x[7], w_ref[10])
    x[5] = y_ref[5] + times_t(x[3], w_ref[8]) + times_t(x[7], w_ref[9])
    x[1] = y_ref[1] + times_t(x[3], w_ref[7])
    x[0] = y_ref[0] + times_t(x[1], w_ref[0])
    for m in (2, 4, 6):
        x[m] = y_ref[m] + times_t(x[m - 1], w_ref[m - 1]) + times_t(x[m + 1], w_ref[m])
    for m in range(HALF):
        squares = x[m] * x[m]
        total = jnp.sum(squares[:, :N] + squares[:, N:], axis=0, keepdims=True) * (1.0 / N)
        out_ref[jnp.bitwise_xor(m, 3 * right)] = total[0]


def call(kernel, shapes, smem, operands, name):
    vmem = pl.BlockSpec(memory_space=pltpu.VMEM)
    scalar = pl.BlockSpec(memory_space=pltpu.SMEM)
    many = isinstance(shapes, list)
    return pl.pallas_call(
        kernel,
        out_shape=[jax.ShapeDtypeStruct(s, f32) for s in shapes] if many else jax.ShapeDtypeStruct(shapes, f32),
        in_specs=[scalar] * smem + [vmem] * (len(operands) - smem),
        out_specs=[vmem] * len(shapes) if many else vmem,
        compiler_params=pltpu.CompilerParams(vmem_limit_bytes=40 * 2**20),
        name=name,
    )(*operands)


def on_device(energy_level, sigma_real, sigma_width, onsite, coupling, source, mode_strength, mode_shift):
    place = lax.axis_index("transpor")
    right = (place >= HALF).astype(jnp.int32)
    odd = jnp.bitwise_xor(place % 2, right)
    side = jnp.stack([right, odd])
    exchange = functools.partial(
        lax.all_to_all, axis_name="transpor", split_axis=0, concat_axis=0, axis_index_groups=GROUPS, tiled=True
    )

    link, columns = call(prepare_kernel, [(N, N), (HALF, 2 * COLS, N)], 1, (side, coupling, source), "prepare")
    first = exchange(jnp.concatenate([jnp.broadcast_to(link, (HALF, N, N)), columns], axis=1))
    own = call(own_kernel, (PACK, N), 2, (side, energy_level, sigma_real, sigma_width, onsite), "own_inverse")
    blocks = exchange(jnp.broadcast_to(own, (HALF, PACK, N)))
    middle, w, y = call(
        half_kernel,
        [(PACK + 2 * COLS, N), (11, N, 2 * N), (HALF, COLS, 2 * N)],
        1,
        (side, blocks, first),
        "half",
    )
    own_link = first[4, :N]
    sent_link = lax.ppermute(own_link, "transpor", MIRROR)
    other = lax.ppermute(middle, "transpor", MIRROR)
    sums = call(middle_kernel, (HALF, N), 1, (side, middle, other, own_link, sent_link, w, y), "middle")
    density = jnp.sum(exchange(sums), axis=0, keepdims=True)
    return (density, mix(density, mode_strength, mode_shift))


def mix(density, mode_strength, mode_shift):
    energies = lax.axis_size("energy")
    index = lax.axis_index("energy")
    odd = index % 2
    couples = [[e, e + 1] for e in range(0, energies, 2)]

    def fetch(value, chips):
        steps = [(e, e - 2 * chips if e % 2 == 0 else e + 2 * chips) for e in range(energies)]
        return lax.ppermute(value, "energy", [(a, b) for a, b in steps if 0 <= b < energies])

    own = lax.all_gather(density, "energy", axis_index_groups=couples, tiled=True)
    near = jnp.concatenate([own, fetch(own, 1)], axis=0)
    middle = fetch(near, 2)
    far = fetch(middle, 2)
    window = jnp.concatenate([near, middle, far], axis=0)
    row = jnp.arange(window.shape[0], dtype=jnp.int32)
    chip = row // 2
    offset = jnp.where(odd == 1, -chip, chip) * 2 + row % 2
    used = jnp.where((odd == 1) & (chip == 0), 0.0, 1.0)
    target = jnp.arange(2, dtype=jnp.int32)
    distance = jnp.abs(offset[None, :] - target[:, None])
    hits = (distance[None] == mode_shift[:, None, None]).astype(f32)
    weights = jnp.sum(mode_strength[:, None, None] * hits, axis=0) * used
    partial = jnp.sum(weights[:, :, None] * window[None], axis=1)
    both = lax.all_gather(partial, "energy", axis_index_groups=couples)
    return lax.dynamic_slice_in_dim(both[0] + both[1], odd, 1, axis=0)


def solution(mesh):
    placed = (
        P("energy"),
        P("energy", "transpor"),
        P("energy", "transpor"),
        P("transpor", None, None),
        P("transpor", None, None),
        P(None, "energy", "transpor", None, None),
        P(),
        P(),
    )
    return jax.shard_map(
        on_device,
        mesh=mesh,
        in_specs=placed,
        out_specs=(P("energy", "transpor"), P("energy", "transpor")),
        check_vma=False,
    )
```

```python
import functools

import jax
import jax.numpy as jnp
from jax import lax
from jax.experimental import pallas as pl
from jax.experimental.pallas import tpu as pltpu
from jax.sharding import PartitionSpec as P

N = 128
TILES = N // 8
HALF = 8
COLS = 16
PACK = N + 8
broadening = 0.2
prec = lax.Precision.HIGHEST
f32 = jnp.float32

GROUPS = [list(range(8)), [12, 13, 14, 15, 8, 9, 10, 11]]
MIRROR = [(x * 4 + y, (3 - x) * 4 + y) for x in range(4) for y in range(4)]


def dot(a, b, dims=((1,), (0,))):
    return lax.dot_general(a, b, (dims, ((), ())), precision=prec, preferred_element_type=f32)


def lanes_of(v, k):
    return jnp.broadcast_to(v[:, k : k + 1], (8, N))


def row_of(v, k):
    return jnp.broadcast_to(v[k : k + 1, :], (8, N))


def pack(re, im):
    return jnp.concatenate([re, im], axis=1)


def turned(v):
    return pack(-v[:, N:], v[:, :N])


def rows_for(v):
    return jnp.concatenate([v, turned(v)], axis=0)


def flip(v):
    return pack(v[:, :N].T, v[:, N:].T)


def times(a, b):
    return dot(a, rows_for(b))


def times_t(a, b):
    f = jnp.concatenate([pack(b[:, :N], -b[:, N:]), pack(b[:, N:], b[:, :N])], axis=0)
    return dot(a, f, ((1,), (1,)))


def iota(shape, d):
    return lax.broadcasted_iota(jnp.int32, shape, d)


def invert(ms, ahead=2):
    R = [[m[8 * u : 8 * u + 8, :N] for u in range(TILES)] for m in ms]
    I = [[m[8 * u : 8 * u + 8, N:] for u in range(TILES)] for m in ms]
    sub, lane = iota((8, N), 0), iota((8, N), 1)
    zero = jnp.zeros((8, 2 * N), f32)
    for t in range(TILES):
        here = (lane >= 8 * t) & (lane < 8 * t + 8)
        unit = jnp.where(lane == sub + 8 * t, 1.0, 0.0)
        for b in range(len(ms)):
            xr, xi = R[b], I[b]
            dr = [lanes_of(xr[t], 8 * t + j) for j in range(8)]
            di = [lanes_of(xi[t], 8 * t + j) for j in range(8)]
            soon = range(t + 1, min(t + 1 + ahead, TILES))
            lr = {u: [lanes_of(xr[u], 8 * t + j) for j in range(8)] for u in soon}
            li = {u: [lanes_of(xi[u], 8 * t + j) for j in range(8)] for u in soon}
            pr = jnp.where(here, unit, xr[t])
            pi = jnp.where(here, 0.0, xi[t])
            for k in range(8):
                p_r, p_i = row_of(dr[k], k), row_of(di[k], k)
                scale = 1.0 / (p_r * p_r + p_i * p_i)
                ir, ii = p_r * scale, p_i * scale
                cr = dr[k] - jnp.where(sub == k, 1.0, 0.0)
                ci = di[k]
                fr = cr * ir + ci * ii
                fi = ci * ir - cr * ii
                for j in range(k + 1, 8):
                    br, bi = row_of(dr[j], k), row_of(di[j], k)
                    dr[j] = dr[j] - fr * br + fi * bi
                    di[j] = di[j] - fr * bi - fi * br
                br, bi = row_of(pr, k), row_of(pi, k)
                pr = pr - fr * br + fi * bi
                pi = pi - fr * bi - fi * br
            new = {t: (pr, pi)}
            for u in soon:
                yr = jnp.where(here, 0.0, xr[u])
                yi = jnp.where(here, 0.0, xi[u])
                for j in range(8):
                    br, bi = row_of(pr, j), row_of(pi, j)
                    yr = yr - lr[u][j] * br + li[u][j] * bi
                    yi = yi - lr[u][j] * bi - li[u][j] * br
                new[u] = (yr, yi)
            rest = [u for u in range(TILES) if u not in new]
            left = jnp.concatenate([pack(xr[u], xi[u]) for u in rest], 0)
            top = [pack(pr, pi) if u == t else zero for u in range(TILES)]
            low = [pack(-pi, pr) if u == t else zero for u in range(TILES)]
            delta = dot(left, jnp.concatenate(top + low, 0))
            for q, u in enumerate(rest):
                new[u] = (
                    jnp.where(here, 0.0, xr[u]) - delta[8 * q : 8 * q + 8, :N],
                    jnp.where(here, 0.0, xi[u]) - delta[8 * q : 8 * q + 8, N:],
                )
            R[b] = [new[u][0] for u in range(TILES)]
            I[b] = [new[u][1] for u in range(TILES)]
    return [jnp.concatenate([pack(r, i) for r, i in zip(R[b], I[b])], 0) for b in range(len(ms))]


def fold(m):
    re, im = m[:, :N], m[:, N:]
    i, j = iota((N, N), 0), iota((N, N), 1)
    diagonal = jnp.sum(jnp.where(i == j, im, 0.0), axis=0, keepdims=True)
    return jnp.concatenate([jnp.where(i >= j, re, im), jnp.broadcast_to(diagonal, (8, N))], axis=0)


def unfold(v):
    a, diagonal = v[:N], v[N : N + 1]
    i, j = iota((N, N), 0), iota((N, N), 1)
    at = a.T
    re = jnp.where(i >= j, a, at)
    im = jnp.where(i == j, diagonal, jnp.where(i < j, a, at))
    return pack(re, im)


def sides():
    place = lax.axis_index("transpor")
    right = (place >= HALF).astype(jnp.int32)
    return right, jnp.bitwise_xor(lax.rem(place, 2), right) == 0


def own_kernel(*refs):
    inputs, out_ref, held, arrived = refs[:6], refs[6], refs[7:13], refs[13]
    copies = [pltpu.make_async_copy(a, b, arrived.at[k]) for k, (a, b) in enumerate(zip(inputs, held))]
    for copy in copies:
        copy.start()
    for copy in copies:
        copy.wait()
    energy_ref, shift_ref, width_ref, onsite_ref, coupling_ref, source_ref = held
    right, first = sides()
    i, j = iota((N, N), 0), iota((N, N), 1)
    re = jnp.where(i == j, energy_ref[...] - shift_ref[...], 0.0) - onsite_ref[0]
    im = jnp.where(i == j, broadening + width_ref[...], 0.0)
    block = pack(re, im)
    link = coupling_ref[0]
    link = jnp.where(right == 1, link.T, link)
    flipped = [source_ref[part, 0, 0].T for part in range(2)]
    for q in range(HALF):
        out_ref[q, PACK : PACK + N] = link
        for part in range(2):
            row = PACK + N + COLS * part
            out_ref[q, row : row + COLS] = flipped[part][COLS * q : COLS * (q + 1)]
    value = fold(jnp.where(first, invert([block])[0], block))
    for q in range(HALF):
        out_ref[q, :PACK] = value


def half_kernel(got_ref, mid_ref, w_ref, y_ref):
    right, _ = sides()
    place = [jnp.bitwise_xor(m, 3 * right) for m in range(HALF)]
    link_place = [jnp.where(right == 1, place[m], m + 1) for m in range(HALF - 1)]
    U = [got_ref[link_place[m], PACK : PACK + N] for m in range(HALF - 1)]
    blocks = [unfold(got_ref[place[m], :PACK]) for m in range(HALF)]
    z = [
        pack(got_ref[place[m], PACK + N : PACK + N + COLS], got_ref[place[m], PACK + N + COLS :])
        for m in range(HALF)
    ]
    D = {m: blocks[m] for m in range(1, HALF, 2)}
    UT = [u.T for u in U]
    V = {}
    slot = iter(range(11))

    def keep(w):
        w_ref[next(slot)] = w

    for m in range(0, HALF, 2):
        p = blocks[m]
        stacked = jnp.concatenate([p[:, :N], p[:, N:]], axis=0)
        y_ref[m] = times(z[m], p)
        if m == 0:
            w = dot(stacked, U[0])
            wr = pack(w[:N], w[N:])
        else:
            w = dot(stacked, pack(UT[m - 1], U[m]))
            wl = pack(w[:N, :N], w[N:, :N])
            wr = pack(w[:N, N:], w[N:, N:])
            up = dot(U[m - 1], jnp.concatenate([wl, wr], axis=1))
            D[m - 1] = D[m - 1] - up[:, : 2 * N]
            V[m - 1] = up[:, 2 * N :]
            z[m - 1] = z[m - 1] + times(z[m], wl)
            keep(wl)
        D[m + 1] = D[m + 1] - dot(UT[m], wr)
        z[m + 1] = z[m + 1] + times(z[m], wr)
        keep(wr)

    p1, p5 = invert([D[1], D[5]])
    y_ref[1] = times(z[1], p1)
    y_ref[5] = times(z[5], p5)
    w1r = times(p1, V[1])
    w5l = times(p5, flip(V[3]))
    w5r = times(p5, V[5])
    D[3] = D[3] - times(flip(V[1]), w1r) - times(V[3], w5l)
    V3 = times(V[3], w5r)
    D[7] = D[7] - times(flip(V[5]), w5r)
    z[3] = z[3] + times(z[1], w1r) + times(z[5], w5l)
    z[7] = z[7] + times(z[5], w5r)
    keep(w1r)
    keep(w5l)
    keep(w5r)

    (p3,) = invert([D[3]])
    y_ref[3] = times(z[3], p3)
    w3r = times(p3, V3)
    keep(w3r)
    D[7] = D[7] - times(flip(V3), w3r)
    z[7] = z[7] + times(z[3], w3r)
    mid_ref[:PACK] = fold(D[7])
    mid_ref[PACK : PACK + COLS] = z[7][:, :N]
    mid_ref[PACK + COLS : PACK + 2 * COLS] = z[7][:, N:]
    mid_ref[PACK + 2 * COLS :] = got_ref[4, PACK : PACK + N]


def middle_kernel(mine_ref, other_ref, w_ref, y_ref, out_ref):
    right, _ = sides()
    link = jnp.where(right == 1, mine_ref[PACK + 2 * COLS :], other_ref[PACK + 2 * COLS :])
    U = jnp.where(right == 1, link, link.T)
    UT = jnp.where(right == 1, link.T, link)
    mine = unfold(mine_ref[:PACK])
    z = pack(mine_ref[PACK : PACK + COLS], mine_ref[PACK + COLS : PACK + 2 * COLS])
    z_other = pack(other_ref[PACK : PACK + COLS], other_ref[PACK + COLS : PACK + 2 * COLS])
    (q,) = invert([unfold(other_ref[:PACK])])
    w = dot(jnp.concatenate([q[:, :N], q[:, N:]], axis=0), UT)
    w = pack(w[:N], w[N:])
    z = z + times(z_other, w)
    (s,) = invert([mine - dot(U, w)])
    x = {7: times(z, s)}
    x[3] = y_ref[3] + times_t(x[7], w_ref[10])
    x[5] = y_ref[5] + times_t(x[3], w_ref[8]) + times_t(x[7], w_ref[9])
    x[1] = y_ref[1] + times_t(x[3], w_ref[7])
    x[0] = y_ref[0] + times_t(x[1], w_ref[0])
    for m in (2, 4, 6):
        x[m] = y_ref[m] + times_t(x[m - 1], w_ref[m - 1]) + times_t(x[m + 1], w_ref[m])
    for m in range(HALF):
        squares = x[m] * x[m]
        total = jnp.sum(squares[:, :N] + squares[:, N:], axis=0, keepdims=True) * (1.0 / N)
        out_ref[jnp.bitwise_xor(m, 3 * right)] = total[0]


def call(kernel, shapes, operands, name, streamed=False):
    vmem = pl.BlockSpec(memory_space=pltpu.VMEM)
    many = isinstance(shapes, list)
    extra = {}
    inputs = [vmem] * len(operands)
    if streamed:
        inputs = [pl.BlockSpec(memory_space=pltpu.HBM)] * len(operands)
        held = [pltpu.VMEM(v.shape, f32) for v in operands]
        extra = dict(scratch_shapes=held + [pltpu.SemaphoreType.DMA((len(operands),))])
    return pl.pallas_call(
        kernel,
        out_shape=[jax.ShapeDtypeStruct(s, f32) for s in shapes] if many else jax.ShapeDtypeStruct(shapes, f32),
        in_specs=inputs,
        out_specs=[vmem] * len(shapes) if many else vmem,
        compiler_params=pltpu.CompilerParams(vmem_limit_bytes=(60 if streamed else 40) * 2**20),
        name=name,
        **extra,
    )(*operands)


def on_device(energy_level, sigma_real, sigma_width, onsite, coupling, source, mode_strength, mode_shift):
    exchange = functools.partial(
        lax.all_to_all, axis_name="transpor", split_axis=0, concat_axis=0, axis_index_groups=GROUPS, tiled=True
    )
    operands = (energy_level.reshape(1, 1), sigma_real, sigma_width, onsite, coupling, source)
    got = exchange(call(own_kernel, (HALF, PACK + N + 2 * COLS, N), operands, "own_inverse", True))
    middle, w, y = call(
        half_kernel, [(PACK + 2 * COLS + N, N), (11, N, 2 * N), (HALF, COLS, 2 * N)], (got,), "half"
    )
    other = lax.ppermute(middle, "transpor", MIRROR)
    sums = call(middle_kernel, (HALF, N), (middle, other, w, y), "middle")
    density = jnp.sum(exchange(sums), axis=0, keepdims=True)
    return (density, mix(density, mode_strength, mode_shift))


def mix(density, mode_strength, mode_shift):
    energies = lax.axis_size("energy")
    index = lax.axis_index("energy")
    odd = index % 2
    couples = [[e, e + 1] for e in range(0, energies, 2)]

    def fetch(value, chips):
        steps = [(e, e - 2 * chips if e % 2 == 0 else e + 2 * chips) for e in range(energies)]
        return lax.ppermute(value, "energy", [(a, b) for a, b in steps if 0 <= b < energies])

    own = lax.all_gather(density, "energy", axis_index_groups=couples, tiled=True)
    near = jnp.concatenate([own, fetch(own, 1)], axis=0)
    middle = fetch(near, 2)
    far = fetch(middle, 2)
    window = jnp.concatenate([near, middle, far], axis=0)
    row = jnp.arange(window.shape[0], dtype=jnp.int32)
    chip = row // 2
    offset = jnp.where(odd == 1, -chip, chip) * 2 + row % 2
    used = jnp.where((odd == 1) & (chip == 0), 0.0, 1.0)
    target = jnp.arange(2, dtype=jnp.int32)
    distance = jnp.abs(offset[None, :] - target[:, None])
    hits = (distance[None] == mode_shift[:, None, None]).astype(f32)
    weights = jnp.sum(mode_strength[:, None, None] * hits, axis=0) * used
    partial = jnp.sum(weights[:, :, None] * window[None], axis=1)
    both = lax.all_gather(partial, "energy", axis_index_groups=couples)
    return lax.dynamic_slice_in_dim(both[0] + both[1], odd, 1, axis=0)


def solution(mesh):
    placed = (
        P("energy"),
        P("energy", "transpor"),
        P("energy", "transpor"),
        P("transpor", None, None),
        P("transpor", None, None),
        P(None, "energy", "transpor", None, None),
        P(),
        P(),
    )
    return jax.shard_map(
        on_device,
        mesh=mesh,
        in_specs=placed,
        out_specs=(P("energy", "transpor"), P("energy", "transpor")),
        check_vma=False,
    )
```

```python
import functools

import jax
import jax.numpy as jnp
from jax import lax
from jax.experimental import pallas as pl
from jax.experimental.pallas import tpu as pltpu
from jax.sharding import PartitionSpec as P

N = 128
TILES = N // 8
HALF = 8
COLS = 16
PACK = N + 8
broadening = 0.2
prec = lax.Precision.HIGHEST
column_prec = lax.Precision.HIGH
f32 = jnp.float32

GROUPS = [list(range(8)), [12, 13, 14, 15, 8, 9, 10, 11]]
MIRROR = [(x * 4 + y, (3 - x) * 4 + y) for x in range(4) for y in range(4)]


def dot(a, b, dims=((1,), (0,))):
    by = column_prec if a.shape[0] == COLS else prec
    return lax.dot_general(a, b, (dims, ((), ())), precision=by, preferred_element_type=f32)


def lanes_of(v, k):
    return jnp.broadcast_to(v[:, k : k + 1], (8, N))


def row_of(v, k):
    return jnp.broadcast_to(v[k : k + 1, :], (8, N))


def pack(re, im):
    return jnp.concatenate([re, im], axis=1)


def turned(v):
    return pack(-v[:, N:], v[:, :N])


def rows_for(v):
    return jnp.concatenate([v, turned(v)], axis=0)


def flip(v):
    return pack(v[:, :N].T, v[:, N:].T)


def times(a, b):
    return dot(a, rows_for(b))


def times_t(a, b):
    f = jnp.concatenate([pack(b[:, :N], -b[:, N:]), pack(b[:, N:], b[:, :N])], axis=0)
    return dot(a, f, ((1,), (1,)))


def iota(shape, d):
    return lax.broadcasted_iota(jnp.int32, shape, d)


def invert(ms, ahead=2):
    R = [[m[8 * u : 8 * u + 8, :N] for u in range(TILES)] for m in ms]
    I = [[m[8 * u : 8 * u + 8, N:] for u in range(TILES)] for m in ms]
    sub, lane = iota((8, N), 0), iota((8, N), 1)
    zero = jnp.zeros((8, 2 * N), f32)
    for t in range(TILES):
        here = (lane >= 8 * t) & (lane < 8 * t + 8)
        unit = jnp.where(lane == sub + 8 * t, 1.0, 0.0)
        for b in range(len(ms)):
            xr, xi = R[b], I[b]
            dr = [lanes_of(xr[t], 8 * t + j) for j in range(8)]
            di = [lanes_of(xi[t], 8 * t + j) for j in range(8)]
            soon = range(t + 1, min(t + 1 + ahead, TILES))
            lr = {u: [lanes_of(xr[u], 8 * t + j) for j in range(8)] for u in soon}
            li = {u: [lanes_of(xi[u], 8 * t + j) for j in range(8)] for u in soon}
            pr = jnp.where(here, unit, xr[t])
            pi = jnp.where(here, 0.0, xi[t])
            for k in range(8):
                p_r, p_i = row_of(dr[k], k), row_of(di[k], k)
                scale = 1.0 / (p_r * p_r + p_i * p_i)
                ir, ii = p_r * scale, p_i * scale
                cr = dr[k] - jnp.where(sub == k, 1.0, 0.0)
                ci = di[k]
                fr = cr * ir + ci * ii
                fi = ci * ir - cr * ii
                for j in range(k + 1, 8):
                    br, bi = row_of(dr[j], k), row_of(di[j], k)
                    dr[j] = dr[j] - fr * br + fi * bi
                    di[j] = di[j] - fr * bi - fi * br
                br, bi = row_of(pr, k), row_of(pi, k)
                pr = pr - fr * br + fi * bi
                pi = pi - fr * bi - fi * br
            new = {t: (pr, pi)}
            for u in soon:
                yr = jnp.where(here, 0.0, xr[u])
                yi = jnp.where(here, 0.0, xi[u])
                for j in range(8):
                    br, bi = row_of(pr, j), row_of(pi, j)
                    yr = yr - lr[u][j] * br + li[u][j] * bi
                    yi = yi - lr[u][j] * bi - li[u][j] * br
                new[u] = (yr, yi)
            rest = [u for u in range(TILES) if u not in new]
            left = jnp.concatenate([pack(xr[u], xi[u]) for u in rest], 0)
            top = [pack(pr, pi) if u == t else zero for u in range(TILES)]
            low = [pack(-pi, pr) if u == t else zero for u in range(TILES)]
            delta = dot(left, jnp.concatenate(top + low, 0))
            for q, u in enumerate(rest):
                new[u] = (
                    jnp.where(here, 0.0, xr[u]) - delta[8 * q : 8 * q + 8, :N],
                    jnp.where(here, 0.0, xi[u]) - delta[8 * q : 8 * q + 8, N:],
                )
            R[b] = [new[u][0] for u in range(TILES)]
            I[b] = [new[u][1] for u in range(TILES)]
    return [jnp.concatenate([pack(r, i) for r, i in zip(R[b], I[b])], 0) for b in range(len(ms))]


def fold(m):
    re, im = m[:, :N], m[:, N:]
    i, j = iota((N, N), 0), iota((N, N), 1)
    diagonal = jnp.sum(jnp.where(i == j, im, 0.0), axis=0, keepdims=True)
    return jnp.concatenate([jnp.where(i >= j, re, im), jnp.broadcast_to(diagonal, (8, N))], axis=0)


def unfold(v):
    a, diagonal = v[:N], v[N : N + 1]
    i, j = iota((N, N), 0), iota((N, N), 1)
    at = a.T
    re = jnp.where(i >= j, a, at)
    im = jnp.where(i == j, diagonal, jnp.where(i < j, a, at))
    return pack(re, im)


def sides():
    place = lax.axis_index("transpor")
    right = (place >= HALF).astype(jnp.int32)
    return right, jnp.bitwise_xor(lax.rem(place, 2), right) == 0


def own_kernel(*refs):
    inputs, out_ref, held, arrived = refs[:6], refs[6], refs[7:13], refs[13]
    copies = [pltpu.make_async_copy(a, b, arrived.at[k]) for k, (a, b) in enumerate(zip(inputs, held))]
    for copy in copies:
        copy.start()
    for copy in copies:
        copy.wait()
    energy_ref, shift_ref, width_ref, onsite_ref, coupling_ref, source_ref = held
    right, first = sides()
    i, j = iota((N, N), 0), iota((N, N), 1)
    re = jnp.where(i == j, energy_ref[...] - shift_ref[...], 0.0) - onsite_ref[0]
    im = jnp.where(i == j, broadening + width_ref[...], 0.0)
    block = pack(re, im)
    link = coupling_ref[0]
    link = jnp.where(right == 1, link.T, link)
    flipped = [source_ref[part, 0, 0].T for part in range(2)]
    for q in range(HALF):
        out_ref[q, PACK : PACK + N] = link
        for part in range(2):
            row = PACK + N + COLS * part
            out_ref[q, row : row + COLS] = flipped[part][COLS * q : COLS * (q + 1)]
    value = fold(jnp.where(first, invert([block])[0], block))
    for q in range(HALF):
        out_ref[q, :PACK] = value


def half_kernel(got_ref, mid_ref, w_ref, y_ref):
    right, _ = sides()
    place = [jnp.bitwise_xor(m, 3 * right) for m in range(HALF)]
    link_place = [jnp.where(right == 1, place[m], m + 1) for m in range(HALF - 1)]
    U = [got_ref[link_place[m], PACK : PACK + N] for m in range(HALF - 1)]
    blocks = [unfold(got_ref[place[m], :PACK]) for m in range(HALF)]
    z = [
        pack(got_ref[place[m], PACK + N : PACK + N + COLS], got_ref[place[m], PACK + N + COLS :])
        for m in range(HALF)
    ]
    D = {m: blocks[m] for m in range(1, HALF, 2)}
    UT = [u.T for u in U]
    V = {}
    slot = iter(range(11))

    def keep(w):
        w_ref[next(slot)] = w

    for m in range(0, HALF, 2):
        p = blocks[m]
        stacked = jnp.concatenate([p[:, :N], p[:, N:]], axis=0)
        y_ref[m] = times(z[m], p)
        if m == 0:
            w = dot(stacked, U[0])
            wr = pack(w[:N], w[N:])
        else:
            w = dot(stacked, pack(UT[m - 1], U[m]))
            wl = pack(w[:N, :N], w[N:, :N])
            wr = pack(w[:N, N:], w[N:, N:])
            up = dot(U[m - 1], jnp.concatenate([wl, wr], axis=1))
            D[m - 1] = D[m - 1] - up[:, : 2 * N]
            V[m - 1] = up[:, 2 * N :]
            z[m - 1] = z[m - 1] + times(z[m], wl)
            keep(wl)
        D[m + 1] = D[m + 1] - dot(UT[m], wr)
        z[m + 1] = z[m + 1] + times(z[m], wr)
        keep(wr)

    p1, p5 = invert([D[1], D[5]])
    y_ref[1] = times(z[1], p1)
    y_ref[5] = times(z[5], p5)
    w1r = times(p1, V[1])
    w5l = times(p5, flip(V[3]))
    w5r = times(p5, V[5])
    D[3] = D[3] - times(flip(V[1]), w1r) - times(V[3], w5l)
    V3 = times(V[3], w5r)
    D[7] = D[7] - times(flip(V[5]), w5r)
    z[3] = z[3] + times(z[1], w1r) + times(z[5], w5l)
    z[7] = z[7] + times(z[5], w5r)
    keep(w1r)
    keep(w5l)
    keep(w5r)

    (p3,) = invert([D[3]])
    y_ref[3] = times(z[3], p3)
    w3r = times(p3, V3)
    keep(w3r)
    D[7] = D[7] - times(flip(V3), w3r)
    z[7] = z[7] + times(z[3], w3r)
    mid_ref[:PACK] = fold(D[7])
    mid_ref[PACK : PACK + COLS] = z[7][:, :N]
    mid_ref[PACK + COLS : PACK + 2 * COLS] = z[7][:, N:]
    mid_ref[PACK + 2 * COLS :] = got_ref[4, PACK : PACK + N]


def middle_kernel(mine_ref, other_ref, w_ref, y_ref, out_ref):
    right, _ = sides()
    link = jnp.where(right == 1, mine_ref[PACK + 2 * COLS :], other_ref[PACK + 2 * COLS :])
    U = jnp.where(right == 1, link, link.T)
    UT = jnp.where(right == 1, link.T, link)
    mine = unfold(mine_ref[:PACK])
    z = pack(mine_ref[PACK : PACK + COLS], mine_ref[PACK + COLS : PACK + 2 * COLS])
    z_other = pack(other_ref[PACK : PACK + COLS], other_ref[PACK + COLS : PACK + 2 * COLS])
    (q,) = invert([unfold(other_ref[:PACK])])
    w = dot(jnp.concatenate([q[:, :N], q[:, N:]], axis=0), UT)
    w = pack(w[:N], w[N:])
    z = z + times(z_other, w)
    (s,) = invert([mine - dot(U, w)])
    x = {7: times(z, s)}
    x[3] = y_ref[3] + times_t(x[7], w_ref[10])
    x[5] = y_ref[5] + times_t(x[3], w_ref[8]) + times_t(x[7], w_ref[9])
    x[1] = y_ref[1] + times_t(x[3], w_ref[7])
    x[0] = y_ref[0] + times_t(x[1], w_ref[0])
    for m in (2, 4, 6):
        x[m] = y_ref[m] + times_t(x[m - 1], w_ref[m - 1]) + times_t(x[m + 1], w_ref[m])
    for m in range(HALF):
        squares = x[m] * x[m]
        total = jnp.sum(squares[:, :N] + squares[:, N:], axis=0, keepdims=True) * (1.0 / N)
        out_ref[jnp.bitwise_xor(m, 3 * right)] = total[0]


def call(kernel, shapes, operands, name, streamed=False):
    vmem = pl.BlockSpec(memory_space=pltpu.VMEM)
    many = isinstance(shapes, list)
    extra = {}
    inputs = [vmem] * len(operands)
    if streamed:
        inputs = [pl.BlockSpec(memory_space=pltpu.HBM)] * len(operands)
        held = [pltpu.VMEM(v.shape, f32) for v in operands]
        extra = dict(scratch_shapes=held + [pltpu.SemaphoreType.DMA((len(operands),))])
    return pl.pallas_call(
        kernel,
        out_shape=[jax.ShapeDtypeStruct(s, f32) for s in shapes] if many else jax.ShapeDtypeStruct(shapes, f32),
        in_specs=inputs,
        out_specs=[vmem] * len(shapes) if many else vmem,
        compiler_params=pltpu.CompilerParams(vmem_limit_bytes=(60 if streamed else 40) * 2**20),
        name=name,
        **extra,
    )(*operands)


def on_device(energy_level, sigma_real, sigma_width, onsite, coupling, source, mode_strength, mode_shift):
    exchange = functools.partial(
        lax.all_to_all, axis_name="transpor", split_axis=0, concat_axis=0, axis_index_groups=GROUPS, tiled=True
    )
    operands = (energy_level.reshape(1, 1), sigma_real, sigma_width, onsite, coupling, source)
    got = exchange(call(own_kernel, (HALF, PACK + N + 2 * COLS, N), operands, "own_inverse", True))
    middle, w, y = call(
        half_kernel, [(PACK + 2 * COLS + N, N), (11, N, 2 * N), (HALF, COLS, 2 * N)], (got,), "half"
    )
    other = lax.ppermute(middle, "transpor", MIRROR)
    sums = call(middle_kernel, (HALF, N), (middle, other, w, y), "middle")
    density = jnp.sum(exchange(sums), axis=0, keepdims=True)
    return (density, mix(density, mode_strength, mode_shift))


def mix(density, mode_strength, mode_shift):
    energies = lax.axis_size("energy")
    everywhere = jnp.broadcast_to(density, (energies, N))
    every = lax.all_to_all(everywhere, "energy", 0, 0, tiled=True)
    distance = jnp.abs(jnp.arange(energies, dtype=jnp.int32) - lax.axis_index("energy"))
    hits = (distance[None] == mode_shift[:, None]).astype(f32)
    weights = jnp.sum(mode_strength[:, None] * hits, axis=0)
    return jnp.sum(weights[:, None] * every, axis=0, keepdims=True)


def solution(mesh):
    placed = (
        P("energy"),
        P("energy", "transpor"),
        P("energy", "transpor"),
        P("transpor", None, None),
        P("transpor", None, None),
        P(None, "energy", "transpor", None, None),
        P(),
        P(),
    )
    return jax.shard_map(
        on_device,
        mesh=mesh,
        in_specs=placed,
        out_specs=(P("energy", "transpor"), P("energy", "transpor")),
        check_vma=False,
    )
```

```python
import functools

import jax
import jax.numpy as jnp
from jax import lax
from jax.experimental import pallas as pl
from jax.experimental.pallas import tpu as pltpu
from jax.sharding import PartitionSpec as P

N = 128
TILES = N // 8
HALF = 8
COLS = 16
PACK = N + 8
broadening = 0.2
prec = lax.Precision.HIGHEST
column_prec = lax.Precision.HIGH
f32 = jnp.float32

GROUPS = [list(range(8)), [12, 13, 14, 15, 8, 9, 10, 11]]
MIRROR = [(x * 4 + y, (3 - x) * 4 + y) for x in range(4) for y in range(4)]


def dot(a, b, dims=((1,), (0,))):
    by = column_prec if a.shape[0] == COLS else prec
    return lax.dot_general(a, b, (dims, ((), ())), precision=by, preferred_element_type=f32)


def lanes_of(v, k):
    return jnp.broadcast_to(v[:, k : k + 1], (8, N))


def row_of(v, k):
    return jnp.broadcast_to(v[k : k + 1, :], (8, N))


def pack(re, im):
    return jnp.concatenate([re, im], axis=1)


def turned(v):
    return pack(-v[:, N:], v[:, :N])


def rows_for(v):
    return jnp.concatenate([v, turned(v)], axis=0)


def flip(v):
    return pack(v[:, :N].T, v[:, N:].T)


def times(a, b):
    return dot(a, rows_for(b))


def times_t(a, b):
    f = jnp.concatenate([pack(b[:, :N], -b[:, N:]), pack(b[:, N:], b[:, :N])], axis=0)
    return dot(a, f, ((1,), (1,)))


def iota(shape, d):
    return lax.broadcasted_iota(jnp.int32, shape, d)


def invert(ms, ahead=2):
    R = [[m[8 * u : 8 * u + 8, :N] for u in range(TILES)] for m in ms]
    I = [[m[8 * u : 8 * u + 8, N:] for u in range(TILES)] for m in ms]
    sub, lane = iota((8, N), 0), iota((8, N), 1)
    zero = jnp.zeros((8, 2 * N), f32)
    for t in range(TILES):
        here = (lane >= 8 * t) & (lane < 8 * t + 8)
        unit = jnp.where(lane == sub + 8 * t, 1.0, 0.0)
        for b in range(len(ms)):
            xr, xi = R[b], I[b]
            dr = [lanes_of(xr[t], 8 * t + j) for j in range(8)]
            di = [lanes_of(xi[t], 8 * t + j) for j in range(8)]
            soon = range(t + 1, min(t + 1 + ahead, TILES))
            lr = {u: [lanes_of(xr[u], 8 * t + j) for j in range(8)] for u in soon}
            li = {u: [lanes_of(xi[u], 8 * t + j) for j in range(8)] for u in soon}
            pr = jnp.where(here, unit, xr[t])
            pi = jnp.where(here, 0.0, xi[t])
            for k in range(8):
                p_r, p_i = row_of(dr[k], k), row_of(di[k], k)
                scale = 1.0 / (p_r * p_r + p_i * p_i)
                ir, ii = p_r * scale, p_i * scale
                cr = dr[k] - jnp.where(sub == k, 1.0, 0.0)
                ci = di[k]
                fr = cr * ir + ci * ii
                fi = ci * ir - cr * ii
                for j in range(k + 1, 8):
                    br, bi = row_of(dr[j], k), row_of(di[j], k)
                    dr[j] = dr[j] - fr * br + fi * bi
                    di[j] = di[j] - fr * bi - fi * br
                br, bi = row_of(pr, k), row_of(pi, k)
                pr = pr - fr * br + fi * bi
                pi = pi - fr * bi - fi * br
            new = {t: (pr, pi)}
            for u in soon:
                yr = jnp.where(here, 0.0, xr[u])
                yi = jnp.where(here, 0.0, xi[u])
                for j in range(8):
                    br, bi = row_of(pr, j), row_of(pi, j)
                    yr = yr - lr[u][j] * br + li[u][j] * bi
                    yi = yi - lr[u][j] * bi - li[u][j] * br
                new[u] = (yr, yi)
            rest = [u for u in range(TILES) if u not in new]
            left = jnp.concatenate([pack(xr[u], xi[u]) for u in rest], 0)
            top = [pack(pr, pi) if u == t else zero for u in range(TILES)]
            low = [pack(-pi, pr) if u == t else zero for u in range(TILES)]
            delta = dot(left, jnp.concatenate(top + low, 0))
            for q, u in enumerate(rest):
                new[u] = (
                    jnp.where(here, 0.0, xr[u]) - delta[8 * q : 8 * q + 8, :N],
                    jnp.where(here, 0.0, xi[u]) - delta[8 * q : 8 * q + 8, N:],
                )
            R[b] = [new[u][0] for u in range(TILES)]
            I[b] = [new[u][1] for u in range(TILES)]
    return [jnp.concatenate([pack(r, i) for r, i in zip(R[b], I[b])], 0) for b in range(len(ms))]


def fold(m):
    re, im = m[:, :N], m[:, N:]
    i, j = iota((N, N), 0), iota((N, N), 1)
    diagonal = jnp.sum(jnp.where(i == j, im, 0.0), axis=0, keepdims=True)
    return jnp.concatenate([jnp.where(i >= j, re, im), jnp.broadcast_to(diagonal, (8, N))], axis=0)


def unfold(v):
    a, diagonal = v[:N], v[N : N + 1]
    i, j = iota((N, N), 0), iota((N, N), 1)
    at = a.T
    re = jnp.where(i >= j, a, at)
    im = jnp.where(i == j, diagonal, jnp.where(i < j, a, at))
    return pack(re, im)


def sides():
    place = lax.axis_index("transpor")
    right = (place >= HALF).astype(jnp.int32)
    return right, jnp.bitwise_xor(lax.rem(place, 2), right) == 0


def own_kernel(*refs):
    inputs, out_ref, held, arrived = refs[:6], refs[6], refs[7:13], refs[13]
    copies = [pltpu.make_async_copy(a, b, arrived.at[k]) for k, (a, b) in enumerate(zip(inputs, held))]
    for copy in copies:
        copy.start()
    for copy in copies:
        copy.wait()
    energy_ref, shift_ref, width_ref, onsite_ref, coupling_ref, source_ref = held
    right, first = sides()
    i, j = iota((N, N), 0), iota((N, N), 1)
    re = jnp.where(i == j, energy_ref[...] - shift_ref[...], 0.0) - onsite_ref[0]
    im = jnp.where(i == j, broadening + width_ref[...], 0.0)
    block = pack(re, im)
    link = coupling_ref[0]
    link = jnp.where(right == 1, link.T, link)
    flipped = [source_ref[part, 0, 0].T for part in range(2)]
    for q in range(HALF):
        out_ref[q, PACK : PACK + N] = link
        for part in range(2):
            row = PACK + N + COLS * part
            out_ref[q, row : row + COLS] = flipped[part][COLS * q : COLS * (q + 1)]
    value = fold(jnp.where(first, invert([block])[0], block))
    for q in range(HALF):
        out_ref[q, :PACK] = value


def half_kernel(got_ref, mid_ref, w_ref, y_ref):
    right, _ = sides()
    place = [jnp.bitwise_xor(m, 3 * right) for m in range(HALF)]
    link_place = [jnp.where(right == 1, place[m], m + 1) for m in range(HALF - 1)]
    U = [got_ref[link_place[m], PACK : PACK + N] for m in range(HALF - 1)]
    blocks = [unfold(got_ref[place[m], :PACK]) for m in range(HALF)]
    z = [
        pack(got_ref[place[m], PACK + N : PACK + N + COLS], got_ref[place[m], PACK + N + COLS :])
        for m in range(HALF)
    ]
    D = {m: blocks[m] for m in range(1, HALF, 2)}
    UT = [u.T for u in U]
    V = {}
    slot = iter(range(11))

    def keep(w):
        w_ref[next(slot)] = w

    solved_left, solved_right = {}, {}
    for m in range(0, HALF, 2):
        p = blocks[m]
        stacked = jnp.concatenate([p[:, :N], p[:, N:]], axis=0)
        y_ref[m] = times(z[m], p)
        if m == 0:
            w = dot(stacked, U[0])
            wr = pack(w[:N], w[N:])
        else:
            w = dot(stacked, pack(UT[m - 1], U[m]))
            wl = pack(w[:N, :N], w[N:, :N])
            wr = pack(w[:N, N:], w[N:, N:])
            V[m - 1] = dot(U[m - 1], wr)
            z[m - 1] = z[m - 1] + times(z[m], wl)
            keep(wl)
            solved_left[m - 1] = wl
        z[m + 1] = z[m + 1] + times(z[m], wr)
        keep(wr)
        solved_right[m + 1] = wr
    for m in (1, 3, 5):
        both = jnp.concatenate([solved_right[m], solved_left[m]], axis=0)
        D[m] = D[m] - dot(pack(UT[m - 1], U[m]), both)
    D[7] = D[7] - dot(UT[6], solved_right[7])

    p1, p5 = invert([D[1], D[5]])
    y_ref[1] = times(z[1], p1)
    y_ref[5] = times(z[5], p5)
    w1r = times(p1, V[1])
    w5l = times(p5, flip(V[3]))
    w5r = times(p5, V[5])
    D[3] = D[3] - times(flip(V[1]), w1r) - times(V[3], w5l)
    V3 = times(V[3], w5r)
    D[7] = D[7] - times(flip(V[5]), w5r)
    z[3] = z[3] + times(z[1], w1r) + times(z[5], w5l)
    z[7] = z[7] + times(z[5], w5r)
    keep(w1r)
    keep(w5l)
    keep(w5r)

    (p3,) = invert([D[3]])
    y_ref[3] = times(z[3], p3)
    w3r = times(p3, V3)
    keep(w3r)
    D[7] = D[7] - times(flip(V3), w3r)
    z[7] = z[7] + times(z[3], w3r)
    mid_ref[:PACK] = fold(D[7])
    mid_ref[PACK : PACK + COLS] = z[7][:, :N]
    mid_ref[PACK + COLS : PACK + 2 * COLS] = z[7][:, N:]
    mid_ref[PACK + 2 * COLS :] = got_ref[4, PACK : PACK + N]


def middle_kernel(mine_ref, other_ref, w_ref, y_ref, out_ref):
    right, _ = sides()
    link = jnp.where(right == 1, mine_ref[PACK + 2 * COLS :], other_ref[PACK + 2 * COLS :])
    U = jnp.where(right == 1, link, link.T)
    UT = jnp.where(right == 1, link.T, link)
    mine = unfold(mine_ref[:PACK])
    z = pack(mine_ref[PACK : PACK + COLS], mine_ref[PACK + COLS : PACK + 2 * COLS])
    z_other = pack(other_ref[PACK : PACK + COLS], other_ref[PACK + COLS : PACK + 2 * COLS])
    (q,) = invert([unfold(other_ref[:PACK])])
    w = dot(jnp.concatenate([q[:, :N], q[:, N:]], axis=0), UT)
    w = pack(w[:N], w[N:])
    z = z + times(z_other, w)
    (s,) = invert([mine - dot(U, w)])
    x = {7: times(z, s)}
    x[3] = y_ref[3] + times_t(x[7], w_ref[10])
    x[5] = y_ref[5] + times_t(x[3], w_ref[8]) + times_t(x[7], w_ref[9])
    x[1] = y_ref[1] + times_t(x[3], w_ref[7])
    x[0] = y_ref[0] + times_t(x[1], w_ref[0])
    for m in (2, 4, 6):
        x[m] = y_ref[m] + times_t(x[m - 1], w_ref[m - 1]) + times_t(x[m + 1], w_ref[m])
    for m in range(HALF):
        squares = x[m] * x[m]
        total = jnp.sum(squares[:, :N] + squares[:, N:], axis=0, keepdims=True) * (1.0 / N)
        out_ref[jnp.bitwise_xor(m, 3 * right)] = total[0]


def call(kernel, shapes, operands, name, streamed=False):
    vmem = pl.BlockSpec(memory_space=pltpu.VMEM)
    many = isinstance(shapes, list)
    extra = {}
    inputs = [vmem] * len(operands)
    if streamed:
        inputs = [pl.BlockSpec(memory_space=pltpu.HBM)] * len(operands)
        held = [pltpu.VMEM(v.shape, f32) for v in operands]
        extra = dict(scratch_shapes=held + [pltpu.SemaphoreType.DMA((len(operands),))])
    return pl.pallas_call(
        kernel,
        out_shape=[jax.ShapeDtypeStruct(s, f32) for s in shapes] if many else jax.ShapeDtypeStruct(shapes, f32),
        in_specs=inputs,
        out_specs=[vmem] * len(shapes) if many else vmem,
        compiler_params=pltpu.CompilerParams(vmem_limit_bytes=(60 if streamed else 40) * 2**20),
        name=name,
        **extra,
    )(*operands)


def on_device(energy_level, sigma_real, sigma_width, onsite, coupling, source, mode_strength, mode_shift):
    exchange = functools.partial(
        lax.all_to_all, axis_name="transpor", split_axis=0, concat_axis=0, axis_index_groups=GROUPS, tiled=True
    )
    operands = (energy_level.reshape(1, 1), sigma_real, sigma_width, onsite, coupling, source)
    got = exchange(call(own_kernel, (HALF, PACK + N + 2 * COLS, N), operands, "own_inverse", True))
    middle, w, y = call(
        half_kernel, [(PACK + 2 * COLS + N, N), (11, N, 2 * N), (HALF, COLS, 2 * N)], (got,), "half"
    )
    other = lax.ppermute(middle, "transpor", MIRROR)
    sums = call(middle_kernel, (HALF, N), (middle, other, w, y), "middle")
    density = jnp.sum(exchange(sums), axis=0, keepdims=True)
    return (density, mix(density, mode_strength, mode_shift))


def mix(density, mode_strength, mode_shift):
    energies = lax.axis_size("energy")
    index = lax.axis_index("energy")
    odd = index % 2
    couples = [[e, e + 1] for e in range(0, energies, 2)]

    def fetch(value, chips):
        steps = [(e, e - 2 * chips if e % 2 == 0 else e + 2 * chips) for e in range(energies)]
        return lax.ppermute(value, "energy", [(a, b) for a, b in steps if 0 <= b < energies])

    own = lax.all_gather(density, "energy", axis_index_groups=couples, tiled=True)
    near = jnp.concatenate([own, fetch(own, 1), fetch(own, 2)], axis=0)
    window = jnp.concatenate([near, fetch(near, 3)], axis=0)
    row = jnp.arange(window.shape[0], dtype=jnp.int32)
    chip = row // 2
    offset = jnp.where(odd == 1, -chip, chip) * 2 + row % 2
    used = jnp.where((odd == 1) & (chip == 0), 0.0, 1.0)
    target = jnp.arange(2, dtype=jnp.int32)
    distance = jnp.abs(offset[None, :] - target[:, None])
    hits = (distance[None] == mode_shift[:, None, None]).astype(f32)
    weights = jnp.sum(mode_strength[:, None, None] * hits, axis=0) * used
    partial = jnp.sum(weights[:, :, None] * window[None], axis=1)
    both = lax.all_gather(partial, "energy", axis_index_groups=couples)
    return lax.dynamic_slice_in_dim(both[0] + both[1], odd, 1, axis=0)


def solution(mesh):
    placed = (
        P("energy"),
        P("energy", "transpor"),
        P("energy", "transpor"),
        P("transpor", None, None),
        P("transpor", None, None),
        P(None, "energy", "transpor", None, None),
        P(),
        P(),
    )
    return jax.shard_map(
        on_device,
        mesh=mesh,
        in_specs=placed,
        out_specs=(P("energy", "transpor"), P("energy", "transpor")),
        check_vma=False,
    )
```

```python
import functools

import jax
import jax.numpy as jnp
from jax import lax
from jax.experimental import pallas as pl
from jax.experimental.pallas import tpu as pltpu
from jax.sharding import PartitionSpec as P

N = 128
TILES = N // 8
HALF = 8
COLS = 16
PACK = N + 8
broadening = 0.2
prec = lax.Precision.HIGHEST
column_prec = lax.Precision.HIGH
f32 = jnp.float32

GROUPS = [list(range(8)), [12, 13, 14, 15, 8, 9, 10, 11]]
MIRROR = [(x * 4 + y, (3 - x) * 4 + y) for x in range(4) for y in range(4)]


def dot(a, b, dims=((1,), (0,))):
    by = column_prec if a.shape[0] == COLS else prec
    return lax.dot_general(a, b, (dims, ((), ())), precision=by, preferred_element_type=f32)


def lanes_of(v, k):
    return jnp.broadcast_to(v[:, k : k + 1], (8, N))


def row_of(v, k):
    return jnp.broadcast_to(v[k : k + 1, :], (8, N))


def pack(re, im):
    return jnp.concatenate([re, im], axis=1)


def turned(v):
    return pack(-v[:, N:], v[:, :N])


def rows_for(v):
    return jnp.concatenate([v, turned(v)], axis=0)


def flip(v):
    return pack(v[:, :N].T, v[:, N:].T)


def times(a, b):
    return dot(a, rows_for(b))


def times_t(a, b):
    f = jnp.concatenate([pack(b[:, :N], -b[:, N:]), pack(b[:, N:], b[:, :N])], axis=0)
    return dot(a, f, ((1,), (1,)))


def iota(shape, d):
    return lax.broadcasted_iota(jnp.int32, shape, d)


def invert(ms, ahead=2):
    R = [[m[8 * u : 8 * u + 8, :N] for u in range(TILES)] for m in ms]
    I = [[m[8 * u : 8 * u + 8, N:] for u in range(TILES)] for m in ms]
    sub, lane = iota((8, N), 0), iota((8, N), 1)
    zero = jnp.zeros((8, 2 * N), f32)
    for t in range(TILES):
        here = (lane >= 8 * t) & (lane < 8 * t + 8)
        unit = jnp.where(lane == sub + 8 * t, 1.0, 0.0)
        for b in range(len(ms)):
            xr, xi = R[b], I[b]
            dr = [lanes_of(xr[t], 8 * t + j) for j in range(8)]
            di = [lanes_of(xi[t], 8 * t + j) for j in range(8)]
            soon = range(t + 1, min(t + 1 + ahead, TILES))
            lr = {u: [lanes_of(xr[u], 8 * t + j) for j in range(8)] for u in soon}
            li = {u: [lanes_of(xi[u], 8 * t + j) for j in range(8)] for u in soon}
            pr = jnp.where(here, unit, xr[t])
            pi = jnp.where(here, 0.0, xi[t])
            for k in range(8):
                p_r, p_i = row_of(dr[k], k), row_of(di[k], k)
                scale = 1.0 / (p_r * p_r + p_i * p_i)
                ir, ii = p_r * scale, p_i * scale
                cr = dr[k] - jnp.where(sub == k, 1.0, 0.0)
                ci = di[k]
                fr = cr * ir + ci * ii
                fi = ci * ir - cr * ii
                for j in range(k + 1, 8):
                    br, bi = row_of(dr[j], k), row_of(di[j], k)
                    dr[j] = dr[j] - fr * br + fi * bi
                    di[j] = di[j] - fr * bi - fi * br
                br, bi = row_of(pr, k), row_of(pi, k)
                pr = pr - fr * br + fi * bi
                pi = pi - fr * bi - fi * br
            new = {t: (pr, pi)}
            for u in soon:
                yr = jnp.where(here, 0.0, xr[u])
                yi = jnp.where(here, 0.0, xi[u])
                for j in range(8):
                    br, bi = row_of(pr, j), row_of(pi, j)
                    yr = yr - lr[u][j] * br + li[u][j] * bi
                    yi = yi - lr[u][j] * bi - li[u][j] * br
                new[u] = (yr, yi)
            rest = [u for u in range(TILES) if u not in new]
            left = jnp.concatenate([pack(xr[u], xi[u]) for u in rest], 0)
            top = [pack(pr, pi) if u == t else zero for u in range(TILES)]
            low = [pack(-pi, pr) if u == t else zero for u in range(TILES)]
            delta = dot(left, jnp.concatenate(top + low, 0))
            for q, u in enumerate(rest):
                new[u] = (
                    jnp.where(here, 0.0, xr[u]) - delta[8 * q : 8 * q + 8, :N],
                    jnp.where(here, 0.0, xi[u]) - delta[8 * q : 8 * q + 8, N:],
                )
            R[b] = [new[u][0] for u in range(TILES)]
            I[b] = [new[u][1] for u in range(TILES)]
    return [jnp.concatenate([pack(r, i) for r, i in zip(R[b], I[b])], 0) for b in range(len(ms))]


def fold(m):
    re, im = m[:, :N], m[:, N:]
    i, j = iota((N, N), 0), iota((N, N), 1)
    diagonal = jnp.sum(jnp.where(i == j, im, 0.0), axis=0, keepdims=True)
    return jnp.concatenate([jnp.where(i >= j, re, im), jnp.broadcast_to(diagonal, (8, N))], axis=0)


def unfold(v):
    a, diagonal = v[:N], v[N : N + 1]
    i, j = iota((N, N), 0), iota((N, N), 1)
    at = a.T
    re = jnp.where(i >= j, a, at)
    im = jnp.where(i == j, diagonal, jnp.where(i < j, a, at))
    return pack(re, im)


def sides():
    place = lax.axis_index("transpor")
    right = (place >= HALF).astype(jnp.int32)
    return right, jnp.bitwise_xor(lax.rem(place, 2), right) == 0


def own_kernel(*refs):
    inputs, out_ref, held, arrived = refs[:6], refs[6], refs[7:13], refs[13]
    copies = [pltpu.make_async_copy(a, b, arrived.at[k]) for k, (a, b) in enumerate(zip(inputs, held))]
    for copy in copies:
        copy.start()
    for copy in copies:
        copy.wait()
    energy_ref, shift_ref, width_ref, onsite_ref, coupling_ref, source_ref = held
    right, first = sides()
    i, j = iota((N, N), 0), iota((N, N), 1)
    re = jnp.where(i == j, energy_ref[...] - shift_ref[...], 0.0) - onsite_ref[0]
    im = jnp.where(i == j, broadening + width_ref[...], 0.0)
    block = pack(re, im)
    link = coupling_ref[0]
    link = jnp.where(right == 1, link.T, link)
    flipped = [source_ref[part, 0, 0].T for part in range(2)]
    for q in range(HALF):
        out_ref[q, PACK : PACK + N] = link
        for part in range(2):
            row = PACK + N + COLS * part
            out_ref[q, row : row + COLS] = flipped[part][COLS * q : COLS * (q + 1)]
    value = fold(jnp.where(first, invert([block])[0], block))
    for q in range(HALF):
        out_ref[q, :PACK] = value


def half_kernel(got_ref, mid_ref, own_ref, w_ref, y_ref):
    right, _ = sides()
    place = [jnp.bitwise_xor(m, 3 * right) for m in range(HALF)]
    link_place = [jnp.where(right == 1, place[m], m + 1) for m in range(HALF - 1)]
    U = [got_ref[link_place[m], PACK : PACK + N] for m in range(HALF - 1)]
    blocks = [unfold(got_ref[place[m], :PACK]) for m in range(HALF)]
    z = [
        pack(got_ref[place[m], PACK + N : PACK + N + COLS], got_ref[place[m], PACK + N + COLS :])
        for m in range(HALF)
    ]
    D = {m: blocks[m] for m in range(1, HALF, 2)}
    UT = [u.T for u in U]
    V = {}
    slot = iter(range(11))

    def keep(w):
        w_ref[next(slot)] = w

    for m in range(0, HALF, 2):
        p = blocks[m]
        stacked = jnp.concatenate([p[:, :N], p[:, N:]], axis=0)
        y_ref[m] = times(z[m], p)
        if m == 0:
            w = dot(stacked, U[0])
            wr = pack(w[:N], w[N:])
        else:
            w = dot(stacked, pack(UT[m - 1], U[m]))
            wl = pack(w[:N, :N], w[N:, :N])
            wr = pack(w[:N, N:], w[N:, N:])
            up = dot(U[m - 1], jnp.concatenate([wl, wr], axis=1))
            D[m - 1] = D[m - 1] - up[:, : 2 * N]
            V[m - 1] = up[:, 2 * N :]
            z[m - 1] = z[m - 1] + times(z[m], wl)
            keep(wl)
        D[m + 1] = D[m + 1] - dot(UT[m], wr)
        z[m + 1] = z[m + 1] + times(z[m], wr)
        keep(wr)

    p1, p5 = invert([D[1], D[5]])
    y_ref[1] = times(z[1], p1)
    y_ref[5] = times(z[5], p5)
    w1r = times(p1, V[1])
    w5l = times(p5, flip(V[3]))
    w5r = times(p5, V[5])
    D[3] = D[3] - times(flip(V[1]), w1r) - times(V[3], w5l)
    V3 = times(V[3], w5r)
    D[7] = D[7] - times(flip(V[5]), w5r)
    z[3] = z[3] + times(z[1], w1r) + times(z[5], w5l)
    z[7] = z[7] + times(z[5], w5r)
    keep(w1r)
    keep(w5l)
    keep(w5r)

    (p3,) = invert([D[3]])
    y_ref[3] = times(z[3], p3)
    w3r = times(p3, V3)
    keep(w3r)
    D[7] = D[7] - times(flip(V3), w3r)
    z[7] = z[7] + times(z[3], w3r)

    (q,) = invert([D[7]])
    own_ref[:N] = D[7]
    own_ref[N:] = z[7]

    def send(value, row):
        mid_ref[:PACK] = fold(value)
        mid_ref[PACK : PACK + COLS] = row[:, :N]
        mid_ref[PACK + COLS :] = row[:, N:]

    @pl.when(right == 0)
    def _():
        send(q, times(z[7], q))

    @pl.when(right == 1)
    def _():
        link = got_ref[4, PACK : PACK + N]
        w = real_times(q, link)
        send(dot(link.T, w), times(z[7], w))


def real_times(a, b):
    w = dot(jnp.concatenate([a[:, :N], a[:, N:]], axis=0), b)
    return pack(w[:N], w[N:])


def middle_kernel(own_ref, sent_ref, link_ref, w_ref, y_ref, out_ref, block_ref):
    right, _ = sides()
    sent = unfold(sent_ref[:PACK])
    row = pack(sent_ref[PACK : PACK + COLS], sent_ref[PACK + COLS :])

    @pl.when(right == 0)
    def _():
        block_ref[:N] = own_ref[:N] - sent
        block_ref[N:] = own_ref[N:] + row

    @pl.when(right == 1)
    def _():
        link = link_ref[4, PACK : PACK + N]
        turned_link = link.T
        block_ref[:N] = own_ref[:N] - dot(link, real_times(sent, turned_link))
        stacked = dot(jnp.concatenate([row[:, :N], row[:, N:]], axis=0), turned_link)
        block_ref[N:] = own_ref[N:] + pack(stacked[:COLS], stacked[COLS:])

    (s,) = invert([block_ref[:N]])
    x = {7: times(block_ref[N:], s)}
    x[3] = y_ref[3] + times_t(x[7], w_ref[10])
    x[5] = y_ref[5] + times_t(x[3], w_ref[8]) + times_t(x[7], w_ref[9])
    x[1] = y_ref[1] + times_t(x[3], w_ref[7])
    x[0] = y_ref[0] + times_t(x[1], w_ref[0])
    for m in (2, 4, 6):
        x[m] = y_ref[m] + times_t(x[m - 1], w_ref[m - 1]) + times_t(x[m + 1], w_ref[m])
    for m in range(HALF):
        squares = x[m] * x[m]
        total = jnp.sum(squares[:, :N] + squares[:, N:], axis=0, keepdims=True) * (1.0 / N)
        out_ref[jnp.bitwise_xor(m, 3 * right)] = total[0]


def call(kernel, shapes, operands, name, streamed=False, scratch=None):
    vmem = pl.BlockSpec(memory_space=pltpu.VMEM)
    many = isinstance(shapes, list)
    extra = {}
    inputs = [vmem] * len(operands)
    if scratch:
        extra = dict(scratch_shapes=[pltpu.VMEM(scratch, f32)])
    if streamed:
        inputs = [pl.BlockSpec(memory_space=pltpu.HBM)] * len(operands)
        held = [pltpu.VMEM(v.shape, f32) for v in operands]
        extra = dict(scratch_shapes=held + [pltpu.SemaphoreType.DMA((len(operands),))])
    return pl.pallas_call(
        kernel,
        out_shape=[jax.ShapeDtypeStruct(s, f32) for s in shapes] if many else jax.ShapeDtypeStruct(shapes, f32),
        in_specs=inputs,
        out_specs=[vmem] * len(shapes) if many else vmem,
        compiler_params=pltpu.CompilerParams(vmem_limit_bytes=(60 if streamed else 40) * 2**20),
        name=name,
        **extra,
    )(*operands)


def on_device(energy_level, sigma_real, sigma_width, onsite, coupling, source, mode_strength, mode_shift):
    exchange = functools.partial(
        lax.all_to_all, axis_name="transpor", split_axis=0, concat_axis=0, axis_index_groups=GROUPS, tiled=True
    )
    operands = (energy_level.reshape(1, 1), sigma_real, sigma_width, onsite, coupling, source)
    got = exchange(call(own_kernel, (HALF, PACK + N + 2 * COLS, N), operands, "own_inverse", True))
    middle, own, w, y = call(
        half_kernel,
        [(PACK + 2 * COLS, N), (N + COLS, 2 * N), (11, N, 2 * N), (HALF, COLS, 2 * N)],
        (got,),
        "half",
    )
    sent = lax.ppermute(middle, "transpor", MIRROR)
    sums = call(middle_kernel, (HALF, N), (own, sent, got, w, y), "middle", scratch=(N + COLS, 2 * N))
    density = jnp.sum(exchange(sums), axis=0, keepdims=True)
    return (density, mix(density, mode_strength, mode_shift))


def mix(density, mode_strength, mode_shift):
    energies = lax.axis_size("energy")
    index = lax.axis_index("energy")
    odd = index % 2
    couples = [[e, e + 1] for e in range(0, energies, 2)]

    def fetch(value, chips):
        steps = [(e, e - 2 * chips if e % 2 == 0 else e + 2 * chips) for e in range(energies)]
        return lax.ppermute(value, "energy", [(a, b) for a, b in steps if 0 <= b < energies])

    own = lax.all_gather(density, "energy", axis_index_groups=couples, tiled=True)
    near = jnp.concatenate([own, fetch(own, 1), fetch(own, 2)], axis=0)
    window = jnp.concatenate([near, fetch(near, 3)], axis=0)
    row = jnp.arange(window.shape[0], dtype=jnp.int32)
    chip = row // 2
    offset = jnp.where(odd == 1, -chip, chip) * 2 + row % 2
    used = jnp.where((odd == 1) & (chip == 0), 0.0, 1.0)
    target = jnp.arange(2, dtype=jnp.int32)
    distance = jnp.abs(offset[None, :] - target[:, None])
    hits = (distance[None] == mode_shift[:, None, None]).astype(f32)
    weights = jnp.sum(mode_strength[:, None, None] * hits, axis=0) * used
    partial = jnp.sum(weights[:, :, None] * window[None], axis=1)
    both = lax.all_gather(partial, "energy", axis_index_groups=couples)
    return lax.dynamic_slice_in_dim(both[0] + both[1], odd, 1, axis=0)


def solution(mesh):
    placed = (
        P("energy"),
        P("energy", "transpor"),
        P("energy", "transpor"),
        P("transpor", None, None),
        P("transpor", None, None),
        P(None, "energy", "transpor", None, None),
        P(),
        P(),
    )
    return jax.shard_map(
        on_device,
        mesh=mesh,
        in_specs=placed,
        out_specs=(P("energy", "transpor"), P("energy", "transpor")),
        check_vma=False,
    )
```

```python
import functools

import jax
import jax.numpy as jnp
from jax import lax
from jax.experimental import pallas as pl
from jax.experimental.pallas import tpu as pltpu
from jax.sharding import PartitionSpec as P

N = 128
TILES = N // 8
HALF = 8
COLS = 16
PACK = N + 8
broadening = 0.2
prec = lax.Precision.HIGHEST
column_prec = lax.Precision.HIGH
f32 = jnp.float32

GROUPS = [list(range(8)), [12, 13, 14, 15, 8, 9, 10, 11]]
MIRROR = [(x * 4 + y, (3 - x) * 4 + y) for x in range(4) for y in range(4)]


def dot(a, b, dims=((1,), (0,)), exact=False):
    by = column_prec if a.shape[0] == COLS and not exact else prec
    return lax.dot_general(a, b, (dims, ((), ())), precision=by, preferred_element_type=f32)


def lanes_of(v, k):
    return jnp.broadcast_to(v[:, k : k + 1], (8, N))


def row_of(v, k):
    return jnp.broadcast_to(v[k : k + 1, :], (8, N))


def pack(re, im):
    return jnp.concatenate([re, im], axis=1)


def turned(v):
    return pack(-v[:, N:], v[:, :N])


def rows_for(v):
    return jnp.concatenate([v, turned(v)], axis=0)


def flip(v):
    return pack(v[:, :N].T, v[:, N:].T)


def times(a, b):
    return dot(a, rows_for(b))


def times_t(a, b):
    f = jnp.concatenate([pack(b[:, :N], -b[:, N:]), pack(b[:, N:], b[:, :N])], axis=0)
    return dot(a, f, ((1,), (1,)))


def iota(shape, d):
    return lax.broadcasted_iota(jnp.int32, shape, d)


def invert(ms, ahead=2, rows=None):
    R = [[m[8 * u : 8 * u + 8, :N] for u in range(TILES)] for m in ms]
    I = [[m[8 * u : 8 * u + 8, N:] for u in range(TILES)] for m in ms]
    if rows is not None:
        R[0] += [rows[8 * q : 8 * q + 8, :N] for q in range(COLS // 8)]
        I[0] += [rows[8 * q : 8 * q + 8, N:] for q in range(COLS // 8)]
    sub, lane = iota((8, N), 0), iota((8, N), 1)
    zero = jnp.zeros((8, 2 * N), f32)
    for t in range(TILES):
        here = (lane >= 8 * t) & (lane < 8 * t + 8)
        unit = jnp.where(lane == sub + 8 * t, 1.0, 0.0)
        for b in range(len(ms)):
            xr, xi = R[b], I[b]
            dr = [lanes_of(xr[t], 8 * t + j) for j in range(8)]
            di = [lanes_of(xi[t], 8 * t + j) for j in range(8)]
            soon = range(t + 1, min(t + 1 + ahead, TILES))
            lr = {u: [lanes_of(xr[u], 8 * t + j) for j in range(8)] for u in soon}
            li = {u: [lanes_of(xi[u], 8 * t + j) for j in range(8)] for u in soon}
            pr = jnp.where(here, unit, xr[t])
            pi = jnp.where(here, 0.0, xi[t])
            for k in range(8):
                p_r, p_i = row_of(dr[k], k), row_of(di[k], k)
                scale = 1.0 / (p_r * p_r + p_i * p_i)
                ir, ii = p_r * scale, p_i * scale
                cr = dr[k] - jnp.where(sub == k, 1.0, 0.0)
                ci = di[k]
                fr = cr * ir + ci * ii
                fi = ci * ir - cr * ii
                for j in range(k + 1, 8):
                    br, bi = row_of(dr[j], k), row_of(di[j], k)
                    dr[j] = dr[j] - fr * br + fi * bi
                    di[j] = di[j] - fr * bi - fi * br
                br, bi = row_of(pr, k), row_of(pi, k)
                pr = pr - fr * br + fi * bi
                pi = pi - fr * bi - fi * br
            new = {t: (pr, pi)}
            for u in soon:
                yr = jnp.where(here, 0.0, xr[u])
                yi = jnp.where(here, 0.0, xi[u])
                for j in range(8):
                    br, bi = row_of(pr, j), row_of(pi, j)
                    yr = yr - lr[u][j] * br + li[u][j] * bi
                    yi = yi - lr[u][j] * bi - li[u][j] * br
                new[u] = (yr, yi)
            rest = [u for u in range(len(xr)) if u not in new and (rows is None or u > t)]
            left = jnp.concatenate([pack(xr[u], xi[u]) for u in rest], 0)
            top = [pack(pr, pi) if u == t else zero for u in range(TILES)]
            low = [pack(-pi, pr) if u == t else zero for u in range(TILES)]
            delta = dot(left, jnp.concatenate(top + low, 0), exact=True)
            for q, u in enumerate(rest):
                new[u] = (
                    jnp.where(here, 0.0, xr[u]) - delta[8 * q : 8 * q + 8, :N],
                    jnp.where(here, 0.0, xi[u]) - delta[8 * q : 8 * q + 8, N:],
                )
            R[b] = [new[u][0] if u in new else xr[u] for u in range(len(xr))]
            I[b] = [new[u][1] if u in new else xi[u] for u in range(len(xi))]
    if rows is not None:
        return jnp.concatenate([pack(-r, -i) for r, i in zip(R[0][TILES:], I[0][TILES:])], 0)
    return [jnp.concatenate([pack(r, i) for r, i in zip(R[b], I[b])], 0) for b in range(len(ms))]


def fold(m):
    re, im = m[:, :N], m[:, N:]
    i, j = iota((N, N), 0), iota((N, N), 1)
    diagonal = jnp.sum(jnp.where(i == j, im, 0.0), axis=0, keepdims=True)
    return jnp.concatenate([jnp.where(i >= j, re, im), jnp.broadcast_to(diagonal, (8, N))], axis=0)


def unfold(v):
    a, diagonal = v[:N], v[N : N + 1]
    i, j = iota((N, N), 0), iota((N, N), 1)
    at = a.T
    re = jnp.where(i >= j, a, at)
    im = jnp.where(i == j, diagonal, jnp.where(i < j, a, at))
    return pack(re, im)


def sides():
    place = lax.axis_index("transpor")
    right = (place >= HALF).astype(jnp.int32)
    return right, jnp.bitwise_xor(lax.rem(place, 2), right) == 0


def own_kernel(*refs):
    inputs, out_ref, held, arrived = refs[:6], refs[6], refs[7:13], refs[13]
    copies = [pltpu.make_async_copy(a, b, arrived.at[k]) for k, (a, b) in enumerate(zip(inputs, held))]
    for copy in copies:
        copy.start()
    for copy in copies:
        copy.wait()
    energy_ref, shift_ref, width_ref, onsite_ref, coupling_ref, source_ref = held
    right, first = sides()
    i, j = iota((N, N), 0), iota((N, N), 1)
    re = jnp.where(i == j, energy_ref[...] - shift_ref[...], 0.0) - onsite_ref[0]
    im = jnp.where(i == j, broadening + width_ref[...], 0.0)
    block = pack(re, im)
    link = coupling_ref[0]
    link = jnp.where(right == 1, link.T, link)
    flipped = [source_ref[part, 0, 0].T for part in range(2)]
    for q in range(HALF):
        out_ref[q, PACK : PACK + N] = link
        for part in range(2):
            row = PACK + N + COLS * part
            out_ref[q, row : row + COLS] = flipped[part][COLS * q : COLS * (q + 1)]
    value = fold(jnp.where(first, invert([block])[0], block))
    for q in range(HALF):
        out_ref[q, :PACK] = value


def half_kernel(got_ref, mid_ref, own_ref, w_ref, y_ref):
    right, _ = sides()
    place = [jnp.bitwise_xor(m, 3 * right) for m in range(HALF)]
    link_place = [jnp.where(right == 1, place[m], m + 1) for m in range(HALF - 1)]
    U = [got_ref[link_place[m], PACK : PACK + N] for m in range(HALF - 1)]
    blocks = [unfold(got_ref[place[m], :PACK]) for m in range(HALF)]
    z = [
        pack(got_ref[place[m], PACK + N : PACK + N + COLS], got_ref[place[m], PACK + N + COLS :])
        for m in range(HALF)
    ]
    D = {m: blocks[m] for m in range(1, HALF, 2)}
    UT = [u.T for u in U]
    V = {}
    slot = iter(range(11))

    def keep(w):
        w_ref[next(slot)] = w

    for m in range(0, HALF, 2):
        p = blocks[m]
        stacked = jnp.concatenate([p[:, :N], p[:, N:]], axis=0)
        y_ref[m] = times(z[m], p)
        if m == 0:
            w = dot(stacked, U[0])
            wr = pack(w[:N], w[N:])
        else:
            w = dot(stacked, pack(UT[m - 1], U[m]))
            wl = pack(w[:N, :N], w[N:, :N])
            wr = pack(w[:N, N:], w[N:, N:])
            up = dot(U[m - 1], jnp.concatenate([wl, wr], axis=1))
            D[m - 1] = D[m - 1] - up[:, : 2 * N]
            V[m - 1] = up[:, 2 * N :]
            z[m - 1] = z[m - 1] + times(z[m], wl)
            keep(wl)
        D[m + 1] = D[m + 1] - dot(UT[m], wr)
        z[m + 1] = z[m + 1] + times(z[m], wr)
        keep(wr)

    p1, p5 = invert([D[1], D[5]])
    y_ref[1] = times(z[1], p1)
    y_ref[5] = times(z[5], p5)
    w1r = times(p1, V[1])
    w5l = times(p5, flip(V[3]))
    w5r = times(p5, V[5])
    D[3] = D[3] - times(flip(V[1]), w1r) - times(V[3], w5l)
    V3 = times(V[3], w5r)
    D[7] = D[7] - times(flip(V[5]), w5r)
    z[3] = z[3] + times(z[1], w1r) + times(z[5], w5l)
    z[7] = z[7] + times(z[5], w5r)
    keep(w1r)
    keep(w5l)
    keep(w5r)

    (p3,) = invert([D[3]])
    y_ref[3] = times(z[3], p3)
    w3r = times(p3, V3)
    keep(w3r)
    D[7] = D[7] - times(flip(V3), w3r)
    z[7] = z[7] + times(z[3], w3r)

    (q,) = invert([D[7]])
    own_ref[:N] = D[7]
    own_ref[N:] = z[7]

    def send(value, row):
        mid_ref[:PACK] = fold(value)
        mid_ref[PACK : PACK + COLS] = row[:, :N]
        mid_ref[PACK + COLS :] = row[:, N:]

    @pl.when(right == 0)
    def _():
        send(q, times(z[7], q))

    @pl.when(right == 1)
    def _():
        link = got_ref[4, PACK : PACK + N]
        w = real_times(q, link)
        send(dot(link.T, w), times(z[7], w))


def real_times(a, b):
    w = dot(jnp.concatenate([a[:, :N], a[:, N:]], axis=0), b)
    return pack(w[:N], w[N:])


def middle_kernel(own_ref, sent_ref, link_ref, w_ref, y_ref, out_ref, block_ref):
    right, _ = sides()
    sent = unfold(sent_ref[:PACK])
    row = pack(sent_ref[PACK : PACK + COLS], sent_ref[PACK + COLS :])

    @pl.when(right == 0)
    def _():
        block_ref[:N] = own_ref[:N] - sent
        block_ref[N:] = own_ref[N:] + row

    @pl.when(right == 1)
    def _():
        link = link_ref[4, PACK : PACK + N]
        turned_link = link.T
        block_ref[:N] = own_ref[:N] - dot(link, real_times(sent, turned_link))
        stacked = dot(jnp.concatenate([row[:, :N], row[:, N:]], axis=0), turned_link)
        block_ref[N:] = own_ref[N:] + pack(stacked[:COLS], stacked[COLS:])

    x = {7: invert([block_ref[:N]], rows=block_ref[N:])}
    x[3] = y_ref[3] + times_t(x[7], w_ref[10])
    x[5] = y_ref[5] + times_t(x[3], w_ref[8]) + times_t(x[7], w_ref[9])
    x[1] = y_ref[1] + times_t(x[3], w_ref[7])
    x[0] = y_ref[0] + times_t(x[1], w_ref[0])
    for m in (2, 4, 6):
        x[m] = y_ref[m] + times_t(x[m - 1], w_ref[m - 1]) + times_t(x[m + 1], w_ref[m])
    for m in range(HALF):
        squares = x[m] * x[m]
        total = jnp.sum(squares[:, :N] + squares[:, N:], axis=0, keepdims=True) * (1.0 / N)
        out_ref[jnp.bitwise_xor(m, 3 * right)] = total[0]


def call(kernel, shapes, operands, name, streamed=False, scratch=None):
    vmem = pl.BlockSpec(memory_space=pltpu.VMEM)
    many = isinstance(shapes, list)
    extra = {}
    inputs = [vmem] * len(operands)
    if scratch:
        extra = dict(scratch_shapes=[pltpu.VMEM(scratch, f32)])
    if streamed:
        inputs = [pl.BlockSpec(memory_space=pltpu.HBM)] * len(operands)
        held = [pltpu.VMEM(v.shape, f32) for v in operands]
        extra = dict(scratch_shapes=held + [pltpu.SemaphoreType.DMA((len(operands),))])
    return pl.pallas_call(
        kernel,
        out_shape=[jax.ShapeDtypeStruct(s, f32) for s in shapes] if many else jax.ShapeDtypeStruct(shapes, f32),
        in_specs=inputs,
        out_specs=[vmem] * len(shapes) if many else vmem,
        compiler_params=pltpu.CompilerParams(vmem_limit_bytes=(60 if streamed else 40) * 2**20),
        name=name,
        **extra,
    )(*operands)


def on_device(energy_level, sigma_real, sigma_width, onsite, coupling, source, mode_strength, mode_shift):
    exchange = functools.partial(
        lax.all_to_all, axis_name="transpor", split_axis=0, concat_axis=0, axis_index_groups=GROUPS, tiled=True
    )
    operands = (energy_level.reshape(1, 1), sigma_real, sigma_width, onsite, coupling, source)
    got = exchange(call(own_kernel, (HALF, PACK + N + 2 * COLS, N), operands, "own_inverse", True))
    middle, own, w, y = call(
        half_kernel,
        [(PACK + 2 * COLS, N), (N + COLS, 2 * N), (11, N, 2 * N), (HALF, COLS, 2 * N)],
        (got,),
        "half",
    )
    sent = lax.ppermute(middle, "transpor", MIRROR)
    sums = call(middle_kernel, (HALF, N), (own, sent, got, w, y), "middle", scratch=(N + COLS, 2 * N))
    density = jnp.sum(exchange(sums), axis=0, keepdims=True)
    return (density, mix(density, mode_strength, mode_shift))


def mix(density, mode_strength, mode_shift):
    energies = lax.axis_size("energy")
    index = lax.axis_index("energy")
    odd = index % 2
    couples = [[e, e + 1] for e in range(0, energies, 2)]

    def fetch(value, chips):
        steps = [(e, e - 2 * chips if e % 2 == 0 else e + 2 * chips) for e in range(energies)]
        return lax.ppermute(value, "energy", [(a, b) for a, b in steps if 0 <= b < energies])

    own = lax.all_gather(density, "energy", axis_index_groups=couples, tiled=True)
    near = jnp.concatenate([own, fetch(own, 1), fetch(own, 2)], axis=0)
    window = jnp.concatenate([near, fetch(near, 3)], axis=0)
    row = jnp.arange(window.shape[0], dtype=jnp.int32)
    chip = row // 2
    offset = jnp.where(odd == 1, -chip, chip) * 2 + row % 2
    used = jnp.where((odd == 1) & (chip == 0), 0.0, 1.0)
    target = jnp.arange(2, dtype=jnp.int32)
    distance = jnp.abs(offset[None, :] - target[:, None])
    hits = (distance[None] == mode_shift[:, None, None]).astype(f32)
    weights = jnp.sum(mode_strength[:, None, None] * hits, axis=0) * used
    partial = jnp.sum(weights[:, :, None] * window[None], axis=1)
    both = lax.all_gather(partial, "energy", axis_index_groups=couples)
    return lax.dynamic_slice_in_dim(both[0] + both[1], odd, 1, axis=0)


def solution(mesh):
    placed = (
        P("energy"),
        P("energy", "transpor"),
        P("energy", "transpor"),
        P("transpor", None, None),
        P("transpor", None, None),
        P(None, "energy", "transpor", None, None),
        P(),
        P(),
    )
    return jax.shard_map(
        on_device,
        mesh=mesh,
        in_specs=placed,
        out_specs=(P("energy", "transpor"), P("energy", "transpor")),
        check_vma=False,
    )
```
